32 devices in a mesh: seq: 8 (over z, y), batch: 4 (over x, core).
Axes of the slice: x: 2, y: 2, z: 4, core: 2. Of those that a mesh axis runs over, the one named last changes fastest.
Arguments:
- tokens: bfloat16 [4, 4096, 1536], P('batch', 'seq'), may hold values from -24 to 24
- filter_tap_weight: float32 [5, 1536], replicated, may hold values from -2.4 to 2.4
- norm_gain: float32 [1536], replicated, may hold values from 0.5 to 1.5
- query_weight: bfloat16 [1536, 512], replicated, may hold values from -4 to 4
- keyval_weight: bfloat16 [1536, 320], replicated, may hold values from -1 to 1
- head_weight: bfloat16 [768, 2, 384], replicated, may hold values from -0.21875 to 0.21875
- head_bias: float32 [2, 384], replicated, may hold values from -1 to 1
- exon_start: int32 [4, 32, 8], P('batch'), may hold values from 0 to 4095, as said below
- exon_end: int32 [4, 32, 8], P('batch'), may hold values from 0 to 4096, as said below
- gene_strand: int32 [4, 32], P('batch'), may hold values from 0 to 1
- gene_owner: int32 [4, 32, 1], P('batch'), may hold values from 0 to 3; in each aligned block of 32 rows (0 to 31, 32 to 63, ..., all dimensions but the last counted through in order) at most 16 rows name the same one
- gene_target: float32 [4, 4, 16, 384], P('batch'), may hold values from 0 to 4
Outputs:
- coverage: bfloat16 [4, 4096, 2, 384], P('batch', 'seq')
- gene_pred: float32 [4, 4, 16, 384], P('batch')
- head_grad: float32 [768, 2, 384], replicated
- bias_grad: float32 [2, 384], replicated
The draws below stay inside these ranges and needn't reach their ends.
Inputs may be any that keep to these rules, and one draw needn't show every extreme that they name: `exon_start`: exons of a gene lie inside the window in increasing order without intersection, each of 1 to 4 bins; unused exon slots have start equal to end; every gene has at least one exon. `exon_end`: as exon_start. `gene_owner`: at most 16 genes of one window have the same owner.
All inputs are finite; a program needn't handle non-finite values.
Results may differ from the reference program's by a relative error of at most 0.025.
Values may be sent and summed in bfloat16 or wider, within the bound.
A program may use at most 64 MiB of HBM per device.

```python
import math
import jax
import jax.numpy as jnp
import numpy as np
from jax import lax

C = 1536
HEADS = 4
DK = 128
DV = 192
TRK = 384
FILTER_TAP_COUNT = 5
DILATION_STRIDE = 64
EXLEN = 4
EXONS = 8
ROWS = 512
GENES = 32
WINDOW_BIN_COUNT = 4096
WINDOWS = 4
CAP = 16
N_BATCH = 4


def exon_bounds(key):
    band = WINDOW_BIN_COUNT // (2 * EXONS)
    span_bins = EXONS * band
    first_key, live_key, size_key, shift_key = jax.random.split(jax.random.fold_in(key, 7), 4)
    shape_full = (WINDOWS, GENES, EXONS)
    gene_index = jnp.arange(GENES, dtype=jnp.int32)[None, :, None]
    exon_index = jnp.arange(EXONS, dtype=jnp.int32)[None, None, :]
    begins = jax.random.randint(first_key, (WINDOWS, GENES, 1), 0, WINDOW_BIN_COUNT - span_bins + 1, dtype=jnp.int32)
    begins = jnp.where(gene_index == 0, 0, jnp.where(gene_index == 1, WINDOW_BIN_COUNT - span_bins, begins)).astype(jnp.int32)
    live_count = jax.random.randint(live_key, (WINDOWS, GENES, 1), 1, EXONS + 1, dtype=jnp.int32)
    live_count = jnp.where(gene_index == 1, EXONS, live_count).astype(jnp.int32)
    sizes = jax.random.randint(size_key, shape_full, 1, EXLEN + 1, dtype=jnp.int32)
    room_left = band - sizes
    shifts = jax.random.randint(shift_key, shape_full, 0, room_left + 1, dtype=jnp.int32)
    shifts = jnp.where((gene_index == 0) & (exon_index == 0), 0, shifts)
    shifts = jnp.where((gene_index == 1) & (exon_index == EXONS - 1), room_left, shifts).astype(jnp.int32)
    starts = begins + exon_index * band + shifts
    used = exon_index < live_count
    return (jnp.where(used, starts, begins).astype(jnp.int32), jnp.where(used, starts + sizes, begins).astype(jnp.int32))


def draw_exon_start(key, part):
    return exon_bounds(key)[0]


def draw_exon_end(key, part):
    return exon_bounds(key)[1]


def attention_weights(key):
    base_key, query_key = jax.random.split(jax.random.fold_in(key, 11), 2)
    keyval = jax.random.truncated_normal(base_key, -6.0, 6.0, (C, DK + DV), jnp.float32) * C ** (-0.5)
    noise = jax.random.truncated_normal(query_key, -6.0, 6.0, (C, HEADS, DK), jnp.float32)
    query = 3.0 * C ** (-0.5) * noise
    return (jnp.clip(query.reshape(C, HEADS * DK), -4.0, 4.0), keyval)


def draw_query_weight(key, part):
    return attention_weights(key)[0].astype(jnp.bfloat16)


def draw_keyval_weight(key, part):
    return attention_weights(key)[1].astype(jnp.bfloat16)


def draw_tokens(key, part):
    base_key = jax.random.fold_in(jax.random.fold_in(key, 3), 0)
    return jax.random.truncated_normal(base_key, -6.0, 6.0, (WINDOWS, WINDOW_BIN_COUNT, C), jnp.float32).astype(jnp.bfloat16)


def touch_ends(values, own_key, low, largest):
    dims = values.shape
    index_at = [jax.random.randint(jax.random.fold_in(own_key, axis), (), 0, dims[axis]) for axis in range(len(dims))]
    values = values.at[tuple(index_at)].set(low)
    longest = dims.index(max(dims))
    index_at[longest] = (index_at[longest] + 1) % dims[longest]
    return values.at[tuple(index_at)].set(largest)


def steps_of(key, dims, cuts, least, top_value):
    gain, own = 1.0, jax.random.fold_in(key, 6)
    for dim, blocks in cuts:
        draws = jnp.exp(jax.random.uniform(jax.random.fold_in(own, dim), (blocks,), jnp.float32, least / len(cuts), top_value / len(cuts)))
        gain = gain * jnp.repeat(draws, dims[dim] // blocks).reshape([-1 if axis == dim else 1 for axis in range(len(dims))])
    return gain


def deal_out(own_key, own, number, rows, number_of, top, bound, slope):
    ranking = jax.random.permutation(own_key, number_of)
    packed, common = portions_of(number_of, rows * top, bound, slope, True), portions_of(number_of, rows * top, bound, slope, False)
    places = jnp.arange(number_of)

    def named(sizes, offset_by):
        used = int((sizes > 0).sum())
        fixed = max(1, used // 4)
        passed = fixed + (places - fixed + offset_by * (used - fixed)) % max(1, number_of - fixed)
        return jnp.zeros((number_of,), jnp.int32).at[ranking[jnp.where(places < fixed, places, passed)]].set(jnp.asarray(sizes, jnp.int32))

    sizes = jnp.where(number % 4 == 0, named(packed, number // 4), named(common, number - number // 4 - 1))
    mixed = jax.random.permutation(jax.random.fold_in(own, 3), number_of)
    donor, receiver = mixed[0:number_of // 2 * 2:2], mixed[1:number_of // 2 * 2:2]
    room = jnp.minimum(sizes[donor] - 1, bound - sizes[receiver]) // 2
    room = jnp.where((donor == ranking[0]) | (receiver == ranking[0]) | (sizes[receiver] == 0), 0, jnp.maximum(room, 0))
    passed = jax.random.randint(jax.random.fold_in(own, 4), (number_of // 2,), 0, 1 << 20) % (room + 1)
    sizes = sizes.at[donor].add(-passed).at[receiver].add(passed)
    items = jnp.searchsorted(jnp.cumsum(sizes), jnp.arange(rows * top), side="right").astype(jnp.int32)
    listing = items.reshape(top, rows).T
    listing = listing[jax.random.permutation(jax.random.fold_in(own, 1), rows)]
    offset_by = jax.random.randint(jax.random.fold_in(own, 2), (rows, 1), 0, top)
    return jnp.take_along_axis(listing, (jnp.arange(top)[None, :] + offset_by) % top, axis=1)


def portions_of(number_of, total, most, lean, full):
    portions = [(1 << 20) // math.isqrt(rank ** lean) + 1 for rank in range(1, number_of + 1)]
    largest = most if full else min(most, max(-(-total // number_of), total * portions[0] // sum(portions)))
    least = 1 if total - largest >= number_of - 1 else 0
    holding, surplus = [largest] + [least] * (number_of - 1), total - largest - least * (number_of - 1)
    while surplus > 0:
        movable = [i for i in range(1, number_of) if holding[i] < largest] or [i for i in range(1, number_of) if holding[i] < most]
        pool, budget = sum([portions[i] for i in movable]), surplus
        for i in movable:
            addition = min(most - holding[i], max(1, budget * portions[i] // pool), surplus)
            holding[i] = holding[i] + addition
            surplus = surplus - addition
    return np.array(holding)


def gaussian(rng, dims, scale, bound, held_as=jnp.bfloat16):
    drawn = scale * jax.random.normal(rng, dims, jnp.float32)
    return jnp.clip(drawn, min=-bound, max=bound).astype(held_as)


def setup_inputs(seed: int = 0) -> dict:
    seeds = jax.random.split(jax.random.key(seed), 13)
    tokens = draw_tokens(jax.random.fold_in(seeds[12], 71), 0)
    filter_tap_weight = gaussian(seeds[1], (FILTER_TAP_COUNT, C), 0.4, 2.4, jnp.float32)
    norm_gain = jnp.clip(1.0 + 0.1 * jax.random.normal(seeds[2], (C,), jnp.float32), 0.5, 1.5)
    query_weight = draw_query_weight(jax.random.fold_in(seeds[12], 71), 0)
    keyval_weight = draw_keyval_weight(jax.random.fold_in(seeds[12], 71), 0)
    head_weight = gaussian(seeds[5], (HEADS * DV, 2, TRK), (HEADS * DV) ** -0.5, 0.21875)
    head_bias = jnp.clip(jax.random.uniform(seeds[6], (2, TRK), jnp.float32, -1.0, 1.0), -1.0, 1.0)
    exon_start = draw_exon_start(jax.random.fold_in(seeds[12], 71), 0)
    exon_end = draw_exon_end(jax.random.fold_in(seeds[12], 71), 0)
    gene_strand = touch_ends(jax.random.randint(seeds[9], (WINDOWS, GENES), 0, 2), jax.random.fold_in(seeds[9], 1), 0, 1).astype(jnp.int32)
    gene_owner_keys = jax.random.split(jax.random.fold_in(seeds[10], 1), WINDOWS * GENES // GENES)
    gene_owner_turns = jax.random.permutation(jax.random.fold_in(seeds[10], 3), WINDOWS * GENES // GENES)
    gene_owner = jax.vmap(lambda own, number: deal_out(jax.random.fold_in(seeds[10], 2), own, number, GENES, N_BATCH, 1, CAP, 2))(gene_owner_keys, gene_owner_turns).reshape((WINDOWS, GENES, 1))
    gene_target = jnp.clip(4.0 * jax.random.uniform(seeds[11], (N_BATCH, WINDOWS, CAP, TRK), jnp.float32) ** steps_of(seeds[11], (N_BATCH, WINDOWS, CAP, TRK), ((0, 4),), -0.2, 0.2), 0.0, 4.0)
    return dict(tokens=tokens, filter_tap_weight=filter_tap_weight, norm_gain=norm_gain, query_weight=query_weight, keyval_weight=keyval_weight, head_weight=head_weight, head_bias=head_bias, exon_start=exon_start, exon_end=exon_end, gene_strand=gene_strand, gene_owner=gene_owner, gene_target=gene_target)


def as_float(values_in):
    return lax.optimization_barrier(values_in).astype(jnp.float32)

def mix_window(tokens_w, filter_tap_weight, norm_gain):
    dilation_reach_rows = FILTER_TAP_COUNT // 2 * DILATION_STRIDE
    widened = tokens_w.astype(jnp.float32)
    zero_extended = jnp.pad(widened, ((dilation_reach_rows, dilation_reach_rows), (0, 0)))
    tap_total = widened
    for filter_tap_index in range(FILTER_TAP_COUNT):
        tap_total = tap_total + filter_tap_weight[filter_tap_index] * zero_extended[filter_tap_index * DILATION_STRIDE:filter_tap_index * DILATION_STRIDE + WINDOW_BIN_COUNT]
    spread = lax.optimization_barrier(jnp.mean(tap_total * tap_total, axis=-1, keepdims=True))
    return (tap_total * lax.rsqrt(spread + 1e-06) * norm_gain).astype(jnp.bfloat16)

def attend_window(normed, query_weight, keyval_weight):
    queries = jnp.dot(normed, query_weight, preferred_element_type=jnp.float32).astype(jnp.bfloat16)
    keyval = jnp.dot(normed, keyval_weight, preferred_element_type=jnp.float32)
    key_rows = as_float(keyval[:, :DK].astype(jnp.bfloat16))
    value_rows = as_float(keyval[:, DK:].astype(jnp.bfloat16))
    query_blocks = queries.reshape(WINDOW_BIN_COUNT // ROWS, ROWS, HEADS, DK)

    def attend_block(query_block):
        scores = jnp.einsum('qhd,kd->qhk', as_float(query_block), key_rows) * DK ** (-0.5)
        row_max = lax.optimization_barrier(jnp.max(scores, axis=-1, keepdims=True))
        weights = jnp.exp(scores - row_max)
        totals = lax.optimization_barrier(jnp.sum(weights, axis=-1, keepdims=True))
        blended = jnp.einsum('qhk,kd->qhd', as_float(weights.astype(jnp.bfloat16)), value_rows) / totals
        return blended.reshape(ROWS, HEADS * DV).astype(jnp.bfloat16)
    return lax.map(attend_block, query_blocks).reshape(WINDOW_BIN_COUNT, HEADS * DV)

def window_pass(tokens_w, start_w, end_w, strand_w, filter_tap_weight, norm_gain, query_weight, keyval_weight, head_weight, head_bias):
    normed = mix_window(tokens_w, filter_tap_weight, norm_gain)
    attended = attend_window(normed, query_weight, keyval_weight)
    logits = jnp.dot(attended, head_weight.reshape(HEADS * DV, 2 * TRK), preferred_element_type=jnp.float32) + head_bias.reshape(2 * TRK)
    coverage = jax.nn.softplus(logits).astype(jnp.bfloat16).reshape(WINDOW_BIN_COUNT, 2, TRK)
    positions = jnp.arange(WINDOW_BIN_COUNT, dtype=jnp.int32)
    inside = (positions[None, None, :] >= start_w[:, :, None]) & (positions[None, None, :] < end_w[:, :, None])
    counts = lax.optimization_barrier(jnp.sum(inside.astype(jnp.float32), axis=1))
    pooled = jnp.dot(counts, attended.astype(jnp.float32), precision=lax.Precision.HIGHEST)
    length = lax.optimization_barrier(jnp.sum((end_w - start_w).astype(jnp.float32), axis=1))
    pooled = pooled / length[:, None]
    per_strand = jnp.einsum('gh,hst->gst', pooled, head_weight.astype(jnp.float32), precision=lax.Precision.HIGHEST) + head_bias[None]
    gene_logit = jnp.where(strand_w[:, None] == 0, per_strand[:, 0], per_strand[:, 1])
    return (coverage, gene_logit, pooled)

def reference(tokens, filter_tap_weight, norm_gain, query_weight, keyval_weight, head_weight, head_bias, exon_start, exon_end, gene_strand, gene_owner, gene_target):

    def per_window(window_items):
        return window_pass(window_items[0], window_items[1], window_items[2], window_items[3], filter_tap_weight, norm_gain, query_weight, keyval_weight, head_weight, head_bias)
    coverage, gene_logit, pooled = lax.map(per_window, (tokens, exon_start, exon_end, gene_strand))
    owners = gene_owner[:, :, 0]
    gene_index = jnp.arange(GENES, dtype=jnp.int32)
    earlier = (owners[:, :, None] == owners[:, None, :]) & (gene_index[None, None, :] < gene_index[None, :, None])
    slot_rank = lax.optimization_barrier(jnp.sum(earlier.astype(jnp.int32), axis=2))
    window_index = jnp.broadcast_to(jnp.arange(WINDOWS, dtype=jnp.int32)[:, None], (WINDOWS, GENES))
    gene_pred = jnp.zeros((N_BATCH, WINDOWS, CAP, TRK), jnp.float32).at[owners, window_index, slot_rank].set(jax.nn.softplus(gene_logit))
    gene_slope = (jnp.log1p(gene_pred) - gene_target) / (1.0 + gene_pred)
    logit_grad = gene_slope[owners, window_index, slot_rank] * jax.nn.sigmoid(gene_logit)
    strand_plus = jnp.where(gene_strand[:, :, None] == 0, logit_grad, 0.0)
    strand_minus = jnp.where(gene_strand[:, :, None] == 1, logit_grad, 0.0)
    placed = jnp.stack([strand_plus, strand_minus], axis=2)
    head_grad = jnp.einsum('wgh,wgst->hst', pooled, placed, precision=lax.Precision.HIGHEST)
    bias_grad = lax.optimization_barrier(jnp.sum(placed, axis=(0, 1)))
    return (coverage, gene_pred, head_grad, bias_grad)
```

```python
import functools
import math

import jax
import jax.numpy as jnp
from jax import lax
from jax.experimental import pallas as pl
from jax.experimental.pallas import tpu as pltpu
from jax.sharding import PartitionSpec as P

HEADS = 4
DK = 128
DV = 192
TRK = 384
TAPS = 5
STRIDE = 64
REACH = TAPS // 2 * STRIDE
CHUNK = 128
MESH = pl.DeviceIdType.MESH
F32 = jnp.float32
BF16 = jnp.bfloat16
NT = (((1,), (1,)), ((), ()))


def softplus(x):
    return jnp.maximum(x, 0.0) + jnp.log1p(jnp.exp(-jnp.abs(x)))


def remote(src, dst, send_sem, recv_sem, device):
    return pltpu.make_async_remote_copy(
        src_ref=src,
        dst_ref=dst,
        send_sem=send_sem,
        recv_sem=recv_sem,
        device_id=device,
        device_id_type=MESH,
    )


def ring_place(s, n):
    odd = s % 2
    return (1 - odd) * (s // 2) + odd * (n - 1 - s // 2)


def ring_member(p, n):
    back = p // (n // 2)
    return (1 - back) * (2 * p) + back * (2 * (n - 1 - p) + 1)


def attention_kernel(
    n, tok, taps, gain, wq, wkv, out,
    ext, wq_v, wkv_v, q, kbuf, vbuf, m, l, acc,
    local_sem, halo_send, halo_recv, ring_send, ring_recv,
):
    rows = tok.shape[0]
    s = lax.axis_index("seq")
    p = ring_place(s, n)
    right = ring_member((p + 1) % n, n)
    left = ring_member((p + n - 1) % n, n)

    own = pltpu.make_async_copy(tok, ext.at[pl.ds(REACH, rows)], local_sem.at[0])
    own.start()
    get_kv = pltpu.make_async_copy(wkv, wkv_v, local_sem.at[1])
    get_kv.start()
    get_q = pltpu.make_async_copy(wq, wq_v, local_sem.at[2])
    get_q.start()

    barrier = pltpu.get_barrier_semaphore()
    has_low = s > 0
    has_high = s < n - 1
    for peer in (left, right):
        pl.semaphore_signal(barrier, inc=1, device_id={"seq": peer}, device_id_type=MESH)

    @pl.when(has_low)
    def _():
        pl.semaphore_signal(barrier, inc=1, device_id={"seq": s - 1}, device_id_type=MESH)

    @pl.when(has_high)
    def _():
        pl.semaphore_signal(barrier, inc=1, device_id={"seq": s + 1}, device_id_type=MESH)

    @pl.when(has_low & has_high)
    def _():
        pl.semaphore_wait(barrier, 4)

    @pl.when(jnp.logical_not(has_low & has_high))
    def _():
        pl.semaphore_wait(barrier, 3)

    to_high = remote(
        tok.at[pl.ds(rows - REACH, REACH)], ext.at[pl.ds(0, REACH)],
        halo_send.at[0], halo_recv.at[0], {"seq": (s + 1) % n},
    )
    to_low = remote(
        tok.at[pl.ds(0, REACH)], ext.at[pl.ds(REACH + rows, REACH)],
        halo_send.at[1], halo_recv.at[1], {"seq": (s + n - 1) % n},
    )

    @pl.when(has_high)
    def _():
        to_high.start()

    @pl.when(has_low)
    def _():
        to_low.start()

    @pl.when(jnp.logical_not(has_low))
    def _():
        ext[pl.ds(0, REACH), :] = jnp.zeros((REACH, ext.shape[1]), BF16)

    @pl.when(jnp.logical_not(has_high))
    def _():
        ext[pl.ds(REACH + rows, REACH), :] = jnp.zeros((REACH, ext.shape[1]), BF16)

    m[...] = jnp.full(m.shape, -1e30, F32)
    l[...] = jnp.zeros(l.shape, F32)
    acc[...] = jnp.zeros(acc.shape, F32)

    factor = DK ** (-0.5) * math.log2(math.e)

    def project(base, piece, offset):
        conv = ext[pl.ds(base + 2 * STRIDE, CHUNK), :].astype(F32)
        for k in range(TAPS):
            conv = conv + taps[pl.ds(k, 1), :] * ext[pl.ds(base + k * STRIDE, CHUNK), :].astype(F32)
        spread = jnp.mean(conv * conv, axis=-1, keepdims=True)
        normed = (conv * lax.rsqrt(spread + 1e-06) * gain[...]).astype(BF16)
        kv = jnp.dot(normed, wkv_v[...], preferred_element_type=F32)
        kbuf[p, piece, pl.ds(offset, CHUNK), :] = kv[:, :DK].astype(BF16)
        vbuf[p, piece, :, pl.ds(offset, CHUNK)] = kv[:, DK:].T.astype(BF16)
        qq = (jnp.dot(normed, wq_v[...], preferred_element_type=F32) * factor).astype(BF16)
        for h in range(HEADS):
            q[h, pl.ds(base, CHUNK), :] = qq[:, h * DK : (h + 1) * DK]

    half = n // 2

    def shard_copies(way, step, piece):
        if way == 0:
            origin, peer = (p + n - step) % n, right
        else:
            origin, peer = (p + step) % n, left
        return [
            remote(
                buf.at[origin, piece], buf.at[origin, piece],
                ring_send.at[way, step, piece, j], ring_recv.at[way, step, piece, j],
                {"seq": peer},
            )
            for j, buf in enumerate((kbuf, vbuf))
        ]

    def start(way, step, piece):
        for c in shard_copies(way, step, piece):
            c.start()

    def attend(slot):
        def pair(i, carry):
            heads = [2 * i + j for j in range(2)]
            keys = kbuf[slot].reshape(rows, DK)
            v0, v1 = vbuf[slot, 0], vbuf[slot, 1]
            old = [(q[h], m[h], l[h], acc[h]) for h in heads]
            new = []
            for qh, mo, lo, ao in old:
                st = lax.dot_general(keys, qh, NT, preferred_element_type=F32)
                mn = jnp.maximum(mo, jnp.max(st, axis=0, keepdims=True))
                w = jnp.exp2(st - mn)
                shrink = jnp.exp2(mo - mn)
                ln = lo * shrink + jnp.sum(w, axis=0, keepdims=True)
                wb = w.astype(BF16)
                an = (
                    ao * shrink
                    + jnp.dot(v0, wb[: rows // 2], preferred_element_type=F32)
                    + jnp.dot(v1, wb[rows // 2 :], preferred_element_type=F32)
                )
                new.append((mn, ln, an))
            for h, (mn, ln, an) in zip(heads, new):
                m[h] = mn
                l[h] = ln
                acc[h] = an
            return carry

        lax.fori_loop(0, HEADS // 2, pair, 0)

    own.wait()
    get_kv.wait()
    get_q.wait()

    def inner(i, carry):
        project(pl.multiple_of((i + 1) * CHUNK, CHUNK), 0, pl.multiple_of(i * CHUNK, CHUNK))
        return carry

    lax.fori_loop(0, 2, inner, 0)
    start(0, 0, 0)
    start(1, 0, 0)

    @pl.when(has_low)
    def _():
        to_high.wait_recv()

    @pl.when(has_high)
    def _():
        to_low.wait_recv()

    def outer(i, carry):
        project(pl.multiple_of(i * (rows - CHUNK), CHUNK), 1, pl.multiple_of(i * CHUNK, CHUNK))
        return carry

    lax.fori_loop(0, 2, outer, 0)
    start(0, 0, 1)
    start(1, 0, 1)
    attend(p)

    for step in range(half):
        last = step == half - 1
        ways_pieces = [(0, 0), (1, 0), (0, 1), (1, 1)] if not last else [(0, 0), (1, 1)]
        for way, piece in ways_pieces:
            for c in shard_copies(way, step, piece):
                c.wait_recv()
            nxt = step + 1
            if nxt < half - 1 or (nxt == half - 1 and (way, piece) in ((0, 0), (1, 1))):
                start(way, nxt, piece)
        if not last:
            attend((p + n - 1 - step) % n)
            attend((p + 1 + step) % n)
        else:
            attend((p + half) % n)

    for h in range(HEADS):
        out[pl.ds(h * DV, DV), :] = (acc[h] / l[h]).astype(BF16)

    @pl.when(has_high)
    def _():
        to_high.wait_send()

    @pl.when(has_low)
    def _():
        to_low.wait_send()

    for step in range(half):
        last = step == half - 1
        ways_pieces = [(0, 0), (1, 0), (0, 1), (1, 1)] if not last else [(0, 0), (1, 1)]
        for way, piece in ways_pieces:
            for c in shard_copies(way, step, piece):
                c.wait_send()


def head_kernel(
    n, nb, att, weight, bias, starts, stops, strand, owner, target,
    cov, pred_out, pool_out, placed_out, bias_out,
    tgt_all, meta_all, pool_all, round_send, round_recv,
    local_sem, tgt_send, tgt_recv, meta_send, meta_recv, pool_send, pool_recv, rs_send, rs_recv,
):
    rows = att.shape[1]
    genes = starts.shape[0]
    cap = target.shape[1]
    s = lax.axis_index("seq")
    b = lax.axis_index("batch")
    rounds = n.bit_length() - 1

    keep = pltpu.make_async_copy(target, tgt_all.at[b], local_sem.at[0])
    keep.start()
    barrier = pltpu.get_barrier_semaphore()
    partners = []
    for r in range(rounds):
        bit = 1 << r
        partners.append(s + bit - 2 * bit * ((s // bit) % 2))
    for partner in partners:
        pl.semaphore_signal(barrier, inc=1, device_id={"seq": partner}, device_id_type=MESH)
    for d in range(1, nb):
        pl.semaphore_signal(barrier, inc=1, device_id={"batch": (b + d) % nb}, device_id_type=MESH)

    lane = lax.broadcasted_iota(jnp.int32, (genes, 128), 1)
    meta_all[b] = jnp.where(lane == 0, strand[...], owner[...]).astype(F32)
    spot = s * rows + lax.broadcasted_iota(jnp.int32, (genes, rows), 1)
    counts = jnp.zeros((genes, rows), F32)
    length = jnp.zeros((genes, 1), F32)
    for e in range(starts.shape[1]):
        lo, hi = starts[:, e : e + 1], stops[:, e : e + 1]
        counts = counts + jnp.where((spot >= lo) & (spot < hi), 1.0, 0.0)
        length = length + (hi - lo).astype(F32)
    partial = lax.dot_general(counts.astype(BF16), att[...], NT, preferred_element_type=F32)

    pl.semaphore_wait(barrier, rounds + nb - 1)

    def coverage(i):
        block = att[:, i * CHUNK : (i + 1) * CHUNK].astype(F32).T.astype(BF16)
        logits = jnp.dot(block, weight[...], preferred_element_type=F32) + bias[...]
        cov[pl.ds(i * CHUNK, CHUNK), :] = softplus(logits).astype(BF16)

    todo = list(range(rows // CHUNK))
    early = []
    for r in range(rounds):
        round_send[r] = partial.astype(BF16)
        c = remote(
            round_send.at[r], round_recv.at[r], rs_send.at[r], rs_recv.at[r], {"seq": partners[r]}
        )
        c.start()
        if r == 0:
            for d in range(1, nb):
                peer = {"batch": (b + d) % nb}
                early.append(remote(target, tgt_all.at[b], tgt_send.at[d - 1], tgt_recv.at[d - 1], peer))
                early.append(
                    remote(meta_all.at[b], meta_all.at[b], meta_send.at[d - 1], meta_recv.at[d - 1], peer)
                )
            for e in early:
                e.start()
        if todo:
            coverage(todo.pop(0))
        c.wait()
        partial = round_send[r].astype(F32) + round_recv[r].astype(F32)

    pool_all[b] = (partial / length).astype(BF16)
    late = [
        remote(
            pool_all.at[b], pool_all.at[b], pool_send.at[d - 1], pool_recv.at[d - 1],
            {"batch": (b + d) % nb},
        )
        for d in range(1, nb)
    ]
    for c in late:
        c.start()
    while todo:
        coverage(todo.pop(0))
    keep.wait()
    for c in early:
        c.wait()
    for c in late:
        c.wait()

    pooled = pool_all[...].reshape(nb * genes, HEADS * DV)
    pool_out[...] = pooled
    both = jnp.dot(pooled, weight[...], preferred_element_type=F32) + bias[...]
    total = jnp.zeros((1, 2 * TRK), F32)
    gene_row = lax.broadcasted_iota(jnp.int32, (genes, genes), 0)
    gene_col = lax.broadcasted_iota(jnp.int32, (genes, genes), 1)
    slot_lane = lax.broadcasted_iota(jnp.int32, (genes, nb * cap), 1).astype(F32)
    lane_f = lane.astype(F32)
    for w in range(nb):
        strands = meta_all[w, :, 0:1]
        owners = meta_all[w, :, 1:2]
        hot = jnp.where(owners == lane_f, 1.0, 0.0).astype(BF16)
        same = lax.dot_general(hot, hot, NT, preferred_element_type=F32)
        rank = jnp.sum(jnp.where(gene_col < gene_row, same, 0.0), axis=1, keepdims=True)
        slot = owners * float(cap) + rank
        logit = both[w * genes : (w + 1) * genes]
        logit = jnp.where(strands == 0.0, logit[:, :TRK], logit[:, TRK:])
        pred = softplus(logit)
        table = jnp.where(slot == slot_lane, 1.0, 0.0)
        goals = tgt_all[:, w].reshape(nb * cap, TRK)
        goal = jnp.dot(table, goals, precision=lax.Precision.HIGHEST, preferred_element_type=F32)
        slope = (jnp.log1p(pred) - goal) / (1.0 + pred)
        grad = slope / (1.0 + jnp.exp(-logit))
        placed = jnp.concatenate(
            [jnp.where(strands == 0.0, grad, 0.0), jnp.where(strands == 0.0, 0.0, grad)], axis=1
        )
        placed_out[pl.ds(w * genes, genes), :] = placed.astype(BF16)
        total = total + jnp.sum(placed, axis=0, keepdims=True)
        mine = slot - (b * cap).astype(F32)
        pick = jnp.where((mine == lane_f) & (lane < cap), 1.0, 0.0).T
        records = jnp.dot(pick, pred, precision=lax.Precision.HIGHEST, preferred_element_type=F32)
        pred_out[w] = records[:cap]
    bias_out[...] = total


def local(
    n, nb, tokens, taps, gain, query_weight, keyval_weight, head_weight, head_bias,
    exon_start, exon_end, gene_strand, gene_owner, gene_target,
):
    rows, width = tokens.shape[1:]
    half = n // 2
    hidden = HEADS * DV
    vmem = pl.BlockSpec(memory_space=pltpu.VMEM)
    anywhere = pl.BlockSpec(memory_space=pl.ANY)
    dma = pltpu.SemaphoreType.DMA
    att = pl.pallas_call(
        functools.partial(attention_kernel, n),
        out_shape=jax.ShapeDtypeStruct((hidden, rows), BF16),
        in_specs=[anywhere, vmem, vmem, anywhere, anywhere],
        out_specs=vmem,
        scratch_shapes=[
            pltpu.VMEM((rows + 2 * REACH, width), BF16),
            pltpu.VMEM(query_weight.shape, BF16),
            pltpu.VMEM(keyval_weight.shape, BF16),
            pltpu.VMEM((HEADS, rows, DK), BF16),
            pltpu.VMEM((n, 2, rows // 2, DK), BF16),
            pltpu.VMEM((n, 2, DV, rows // 2), BF16),
            pltpu.VMEM((HEADS, 1, rows), F32),
            pltpu.VMEM((HEADS, 1, rows), F32),
            pltpu.VMEM((HEADS, DV, rows), F32),
            dma((3,)),
            dma((2,)),
            dma((2,)),
            dma((2, half, 2, 2)),
            dma((2, half, 2, 2)),
        ],
        compiler_params=pltpu.CompilerParams(
            collective_id=0, has_side_effects=True, vmem_limit_bytes=44 * 1024 * 1024
        ),
        name="attention",
    )(tokens[0], taps, gain.reshape(1, width), query_weight, keyval_weight)

    genes = exon_start.shape[1]
    cap = gene_target.shape[2]
    rounds = n.bit_length() - 1
    cov, pred, pooled, placed, bias_grad = pl.pallas_call(
        functools.partial(head_kernel, n, nb),
        out_shape=[
            jax.ShapeDtypeStruct((rows, 2 * TRK), BF16),
            jax.ShapeDtypeStruct((nb, cap, TRK), F32),
            jax.ShapeDtypeStruct((nb * genes, hidden), BF16),
            jax.ShapeDtypeStruct((nb * genes, 2 * TRK), BF16),
            jax.ShapeDtypeStruct((1, 2 * TRK), F32),
        ],
        in_specs=[vmem] * 8,
        out_specs=[vmem] * 5,
        scratch_shapes=[
            pltpu.VMEM((nb, nb, cap, TRK), F32),
            pltpu.VMEM((nb, genes, 128), F32),
            pltpu.VMEM((nb, genes, hidden), BF16),
            pltpu.VMEM((rounds, genes, hidden), BF16),
            pltpu.VMEM((rounds, genes, hidden), BF16),
            dma((1,)),
            dma((nb - 1,)),
            dma((nb - 1,)),
            dma((nb - 1,)),
            dma((nb - 1,)),
            dma((nb - 1,)),
            dma((nb - 1,)),
            dma((rounds,)),
            dma((rounds,)),
        ],
        compiler_params=pltpu.CompilerParams(
            collective_id=1, has_side_effects=True, vmem_limit_bytes=44 * 1024 * 1024
        ),
        name="heads",
    )(
        att,
        head_weight.reshape(hidden, 2 * TRK),
        head_bias.reshape(1, 2 * TRK),
        exon_start[0],
        exon_end[0],
        gene_strand.reshape(genes, 1),
        gene_owner[0],
        gene_target[0],
    )
    head_grad = jnp.einsum(
        "gh,gst->hst", pooled, placed.reshape(nb * genes, 2, TRK), preferred_element_type=F32
    )
    return (cov.reshape(1, rows, 2, TRK), pred[None], head_grad, bias_grad.reshape(2, TRK))


def solution(mesh):
    in_specs = (
        P("batch", "seq", None),
        P(),
        P(),
        P(),
        P(),
        P(),
        P(),
        P("batch", None, None),
        P("batch", None, None),
        P("batch", None),
        P("batch", None, None),
        P("batch", None, None, None),
    )
    out_specs = (P("batch", "seq", None, None), P("batch", None, None, None), P(), P())
    body = functools.partial(local, mesh.shape["seq"], mesh.shape["batch"])
    return jax.shard_map(body, mesh=mesh, in_specs=in_specs, out_specs=out_specs, check_vma=False)
```
